128 devices in a mesh: lat: 8 (over x, core), lon: 16 (over y, z).
Axes of the slice: x: 4, y: 4, z: 4, core: 2. Of those that a mesh axis runs over, the one named last changes fastest.
Arguments:
- state: bfloat16 [8, 16, 64, 50, 8, 128], P('lat', 'lon'), may hold values from -6 to 6
- ocean_mask: int32 [8, 16, 64, 8], P('lat', 'lon'), may hold values 0 or 1
- obs_pert: bfloat16 [8, 16, 4096, 128], P('lat', 'lon'), may hold values from -20 to 20
- innovation: float32 [8, 16, 4096], P('lat', 'lon'), may hold values from -6 to 6
- precision: float32 [8, 16, 4096], P('lat', 'lon'), may hold values from 0.25 to 4
- obs_index: int32 [8, 16, 64, 256], P('lat', 'lon'), may hold values from 0 to 36863, as said below
- obs_count: int32 [8, 16, 64], P('lat', 'lon'), may hold values from 0 to 256, as said below
Outputs:
- analysis: bfloat16 [8, 16, 64, 50, 8, 128], P('lat', 'lon')
The draws below stay inside these ranges and needn't reach their ends.
Inputs may be any that keep to these rules, and one draw needn't show every extreme that they name: `obs_index`: an entry (3 u + v) * 4096 + q names row q of the tile at latitude offset u - 1 and longitude offset v - 1 (longitudes periodic); no entry names a tile beyond the first or last row of tiles. `obs_count`: in every row of tiles exactly 512 patches have a nonzero count; the tiles of a row fall into pairs whose observed patches add up to 64, and some tile of every row has all 64 patches observed.
All inputs are finite; a program needn't handle non-finite values. No bound on the sum of `ocean_mask` on one device may be relied on, other than what follows from the above.
Results may differ from the reference program's by a relative error of at most 0.0039.
Values may be sent and summed in bfloat16 or wider, within the bound.
A program may use at most 128 MiB of HBM per device.

```python
import math
import jax
import jax.numpy as jnp
from jax import lax

MEMBERS = 128
LEVELS = 50
COLUMNS = 8
OBS_ROWS = 256
PATCHES = 64
SWEEPS = 8
POOL = 4096
TILES_LAT = 8
TILES_LON = 16
LOAD = 32


def draw_obs_pert(key, part):
    key = jax.random.fold_in(key, 5)
    key_base, key_scale = jax.random.split(key, 2)
    shape = (TILES_LAT, TILES_LON, POOL, MEMBERS)
    base = jnp.clip(jax.random.normal(key_base, shape, jnp.float32), -5.0, 5.0)
    row_scale = jnp.exp(jax.random.uniform(key_scale, (TILES_LAT, TILES_LON, POOL, 1), jnp.float32, math.log(0.3), math.log(3.0)))
    return (row_scale * base).astype(jnp.bfloat16)


def draw_obs_index(key, part):
    key = jax.random.fold_in(key, 12)
    key_lat, key_lon, key_row = jax.random.split(key, 3)
    shape = (TILES_LAT, TILES_LON, PATCHES, OBS_ROWS)
    lat_off = jax.random.randint(key_lat, shape, 0, 3)
    lon_off = jax.random.randint(key_lon, shape, 0, 3)
    pool_row = jax.random.randint(key_row, shape, 0, POOL)
    lat_ids = jnp.arange(TILES_LAT, dtype=jnp.int32)[:, None, None, None]
    lat_off = jnp.where((lat_ids == 0) & (lat_off == 0), 1, lat_off)
    lat_off = jnp.where((lat_ids == TILES_LAT - 1) & (lat_off == 2), 1, lat_off)
    picks = (lat_off * 3 + lon_off) * POOL + pool_row
    picks = picks.at[0, 0, 0, 0].set(9 * POOL - 1)
    picks = picks.at[TILES_LAT - 1, 0, 0, 0].set(0)
    return picks.astype(jnp.int32)


def draw_obs_count(key, part):
    key = jax.random.fold_in(key, 11)
    key_perm, key_high, key_order, key_count = jax.random.split(key, 4)
    perm_keys = jax.random.split(key_perm, TILES_LAT)
    shuffle = jax.vmap(lambda one: jax.random.permutation(one, TILES_LON))(perm_keys)
    high = jax.random.randint(key_high, (TILES_LAT, TILES_LON // 2), LOAD + LOAD // 2, 2 * LOAD + 1)
    high = high.at[:, 0].set(2 * LOAD)
    low = 2 * LOAD - high
    pair_loads = jnp.stack([high, low], axis=-1).reshape(TILES_LAT, TILES_LON)
    inverse_perm = jnp.argsort(shuffle, axis=1)
    tile_loads = jnp.take_along_axis(pair_loads, inverse_perm, axis=1)
    order_keys = jax.random.split(key_order, TILES_LAT * TILES_LON)
    patch_order = jax.vmap(lambda one: jax.random.permutation(one, PATCHES))(order_keys).reshape(TILES_LAT, TILES_LON, PATCHES)
    active = patch_order < tile_loads[:, :, None]
    counts = jax.random.randint(key_count, (TILES_LAT, TILES_LON, PATCHES), OBS_ROWS // 4, OBS_ROWS + 1)
    counts = jnp.where(patch_order == 0, OBS_ROWS, counts)
    return jnp.where(active, counts, 0).astype(jnp.int32)


def touch_ends(result, own_key, smallest, top_value):
    longest = result.shape.index(max(result.shape))
    spots = []
    for shift in (0, 1):
        where = [jax.random.randint(jax.random.fold_in(own_key, axis), (), 0, length) for axis, length in enumerate(result.shape)]
        where[longest] = (where[longest] + shift) % result.shape[longest]
        spots.append(tuple(where))
    return result.at[spots[0]].set(smallest).at[spots[1]].set(top_value)


def level_of(key, shape, cuts, low, high):
    factor_of, own = 1.0, jax.random.fold_in(key, 6)
    for axis_at, parts in cuts:
        steps = jnp.exp(jax.random.uniform(jax.random.fold_in(own, axis_at), (parts,), jnp.float32, low / len(cuts), high / len(cuts)))
        factor_of = factor_of * jnp.repeat(steps, shape[axis_at] // parts).reshape([-1 if axis == axis_at else 1 for axis in range(len(shape))])
    return factor_of


def centred(own_key, shape, scale, bound, cuts=(), kind=jnp.bfloat16):
    drawn = scale * jax.random.normal(own_key, shape, jnp.float32)
    if cuts:
        drawn = drawn * level_of(own_key, shape, cuts, -0.22, 0.18)
    return jnp.clip(drawn, -bound, bound).astype(kind)


def setup_inputs(seed: int = 0) -> dict:
    streams_of = jax.random.split(jax.random.key(seed), 8)
    return {
        "state": centred(streams_of[0], (TILES_LAT, TILES_LON, PATCHES, LEVELS, COLUMNS, MEMBERS), 1.0, 6.0, ((0, 8), (1, 16))),
        "ocean_mask": touch_ends((jax.random.randint(streams_of[1], (TILES_LAT, TILES_LON, PATCHES, COLUMNS), 0, 4) < 3).astype(jnp.int32), jax.random.fold_in(streams_of[1], 1), 0, 1),
        "obs_pert": draw_obs_pert(jax.random.fold_in(streams_of[7], 71), 0),
        "innovation": centred(streams_of[3], (TILES_LAT, TILES_LON, POOL), 1.0, 6.0, ((0, 8), (1, 16)), jnp.float32),
        "precision": jnp.clip(jnp.exp(math.log(4.0) - 2.7725887 * jax.random.uniform(streams_of[4], (TILES_LAT, TILES_LON, POOL), jnp.float32) ** level_of(streams_of[4], (TILES_LAT, TILES_LON, POOL), ((0, 8), (1, 16)), -0.2, 0.2)), 0.25, 4.0),
        "obs_index": draw_obs_index(jax.random.fold_in(streams_of[7], 71), 0),
        "obs_count": draw_obs_count(jax.random.fold_in(streams_of[7], 71), 0),
    }


def weights_of(picked_rows, picked_vals):
    members = picked_rows.shape[-1]
    rows_wide = picked_rows.astype(jnp.float32)
    vals_wide = picked_vals.astype(jnp.float32)
    highest = lax.Precision.HIGHEST
    gram_matrix = jnp.einsum('nlk,nlj->nkj', rows_wide, rows_wide, precision=highest)
    projected = jnp.einsum('nlk,nl->nk', rows_wide, vals_wide, precision=highest)
    identity = jnp.eye(members, dtype=jnp.float32)
    members_less = jnp.float32(members - 1)
    system = identity + gram_matrix / members_less
    frobenius = jnp.sqrt(lax.optimization_barrier(jnp.sum(system * system, axis=(1, 2), keepdims=True)))
    iterate = system / frobenius
    inverse = jnp.broadcast_to(identity, system.shape)
    for sweep in range(SWEEPS):
        update = 1.5 * identity - 0.5 * jnp.matmul(inverse, iterate, precision=highest)
        iterate = jnp.matmul(iterate, update, precision=highest)
        inverse = jnp.matmul(update, inverse, precision=highest)
    root_cov = inverse / jnp.sqrt(frobenius * members_less)
    covariance = jnp.matmul(root_cov, root_cov, precision=highest)
    mean_weight = jnp.einsum('nkj,nj->nk', covariance, projected, precision=highest)
    weights = (jnp.sqrt(members_less) * root_cov + mean_weight[:, :, None]).astype(jnp.bfloat16)
    return lax.optimization_barrier(weights)

def analyse(columns, weights):
    values = columns.astype(jnp.float32)
    center = lax.optimization_barrier(jnp.mean(values, axis=-1, keepdims=True))
    spread = lax.optimization_barrier((values - center).astype(jnp.bfloat16))
    product = jnp.einsum('nabk,nkj->nabj', spread.astype(jnp.float32), weights.astype(jnp.float32), precision=lax.Precision.HIGHEST)
    return center + product

def reference(state, ocean_mask, obs_pert, innovation, precision, obs_index, obs_count):
    root_prec = jnp.sqrt(precision)
    scaled = lax.optimization_barrier((root_prec[..., None] * obs_pert.astype(jnp.float32)).astype(jnp.bfloat16))
    weighted = lax.optimization_barrier((root_prec * innovation).astype(jnp.bfloat16))
    zero_half = jnp.zeros((), jnp.bfloat16)

    def one_tile(tile_id):
        lat_id = tile_id // TILES_LON
        lon_id = tile_id % TILES_LON
        offsets = jnp.arange(3, dtype=jnp.int32) - 1
        lat_rows = jnp.clip(lat_id + offsets, 0, TILES_LAT - 1)
        lon_cols = (lon_id + offsets) % TILES_LON
        ext_rows = scaled[lat_rows[:, None], lon_cols[None, :]].reshape(9 * POOL, MEMBERS)
        ext_vals = weighted[lat_rows[:, None], lon_cols[None, :]].reshape(9 * POOL)
        pick_rows = obs_index[lat_id, lon_id]
        counts = obs_count[lat_id, lon_id]
        in_window = jnp.arange(OBS_ROWS, dtype=jnp.int32)[None, :] < counts[:, None]
        picked_rows = jnp.where(in_window[..., None], ext_rows[pick_rows], zero_half)
        picked_vals = jnp.where(in_window, ext_vals[pick_rows], zero_half)
        weights = weights_of(picked_rows, picked_vals)
        columns = state[lat_id, lon_id]
        analysed = analyse(columns, weights)
        updated = (counts > 0)[:, None, None, None] & (ocean_mask[lat_id, lon_id][:, None, :, None] > 0)
        return jnp.where(updated, analysed, columns.astype(jnp.float32)).astype(jnp.bfloat16)
    tiles = lax.map(one_tile, jnp.arange(TILES_LAT * TILES_LON, dtype=jnp.int32))
    return tiles.reshape(state.shape)
```

```python
import functools
import jax, jax.numpy as jnp
from jax import lax
from jax.sharding import PartitionSpec as P
from jax.experimental import pallas as pl
from jax.experimental.pallas import tpu as pltpu

SWEEPS = 8
f32, bf16 = jnp.float32, jnp.bfloat16

def split(x):
    hi = x.astype(bf16)
    lo = (x - hi.astype(f32)).astype(bf16)
    return hi, lo

def wide(x):
    hi, lo = split(x)
    return jnp.concatenate([hi, lo], axis=1)

def twice(x):
    hi, lo = split(x)
    top = jnp.concatenate([hi, lo], axis=1)
    return jnp.concatenate([top, top], axis=0)

def times(left, right):
    out = jnp.dot(left, right, preferred_element_type=f32)
    half = out.shape[1] // 2
    return out[:, :half] + out[:, half:]

def body(G, CH, idx_ref, *refs):
    tiles = refs[:9]
    vals_ref, upd_ref, state_ref, out_ref, table, picked, stage, mref, zref, sem = refs[9:]
    step = pl.program_id(0)
    members = 128
    pool = tiles[0].shape[0]
    chunks = [(t, c) for t in range(9) for c in range(pool // CH)]

    @pl.when(step == 0)
    def _():
        def fetch(k):
            t, c = chunks[k]
            return pltpu.make_async_copy(tiles[t].at[pl.ds(c * CH, CH)], stage.at[k % 2], sem.at[k % 2])
        fetch(0).start()
        for k in range(len(chunks)):
            if k + 1 < len(chunks):
                fetch(k + 1).start()
            fetch(k).wait()
            t, c = chunks[k]
            base = t * pool + c * CH
            table[pl.ds(base, CH)] = stage[k % 2].astype(f32).reshape(CH, 1, members)
        table[pl.ds(9 * pool, 8)] = jnp.zeros((8, 1, members), f32)

    U = 16
    def gather(i, _):
        for u in range(U):
            r = i * U + u
            picked[pl.ds(r, 1)] = table[pl.ds(idx_ref[step * G * 256 + r], 1)]
        return 0
    lax.fori_loop(0, G * 256 // U, gather, 0)

    rows_i = lax.broadcasted_iota(jnp.int32, (members, members), 0)
    cols_i = lax.broadcasted_iota(jnp.int32, (members, members), 1)
    eye = (rows_i == cols_i).astype(f32)
    frob = []
    proj = []
    for g in range(G):
        rows = picked[pl.ds(g * 256, 256)].reshape(256, members).astype(bf16)
        gram = lax.dot_general(rows, rows, (((0,), (0,)), ((), ())), preferred_element_type=f32)
        pv = jnp.broadcast_to(vals_ref[pl.ds(step * G + g, 1), :], (8, 256)).astype(bf16)
        proj.append(jnp.dot(pv, rows, preferred_element_type=f32))
        system = eye + gram * f32(1.0 / 127.0)
        fr = jnp.sqrt(jnp.sum(system * system, axis=(0, 1), keepdims=True))
        frob.append(fr)
        A = system / fr
        W = twice(-0.5 * A)
        T = 1.5 * A + times(wide(A), W)
        mref[g] = 1.5 * T + times(wide(T), W)
        zref[g] = 1.5 * eye - 0.5 * A

    def sweep(k, _):
        for g in range(G):
            M = mref[g]
            Z = zref[g]
            W = twice(-0.5 * M)
            R = times(jnp.concatenate([wide(M), wide(Z)], axis=0), W)
            T = 1.5 * M + R[:members]
            zref[g] = 1.5 * Z + R[members:]
            mref[g] = 1.5 * T + times(wide(T), W)
        return 0
    lax.fori_loop(0, SWEEPS - 2, sweep, 0)

    for g in range(G):
        M = mref[g]
        Z = zref[g]
        Z = 1.5 * Z + times(wide(Z), twice(-0.5 * M))
        root = Z / jnp.sqrt(frob[g] * f32(127.0))
        Rw = twice(root)
        mw = times(wide(times(wide(proj[g]), Rw)), Rw)
        weights_t = (jnp.sqrt(f32(127.0)) * root + mw[:1]).astype(bf16)
        x = state_ref[g]
        values = x.astype(f32)
        center = jnp.sum(values, axis=-1, keepdims=True) * f32(1.0 / members)
        spread = (values - center).astype(bf16)
        got = center + lax.dot_general(spread, weights_t, (((1,), (1,)), ((), ())), preferred_element_type=f32)
        n = values.shape[0]
        upd = upd_ref[g]
        res = jnp.where(upd[None] > 0, got.reshape(n // 8, 8, members), values.reshape(n // 8, 8, members))
        out_ref[g] = res.reshape(n, members).astype(bf16)

def analyse_patches(idx, tiles, vals, upd, state, G=4, CH=1024):
    N = vals.shape[0]
    pool = tiles[0].shape[0]
    rows = state.shape[1]
    return pl.pallas_call(
        functools.partial(body, G, CH),
        grid_spec=pltpu.PrefetchScalarGridSpec(
            num_scalar_prefetch=1,
            grid=(N // G,),
            in_specs=[pl.BlockSpec(memory_space=pl.ANY)] * 9 + [
                pl.BlockSpec((N, 256), lambda i, s: (0, 0)),
                pl.BlockSpec((G, 8, 128), lambda i, s: (i, 0, 0)),
                pl.BlockSpec((G, rows, 128), lambda i, s: (i, 0, 0)),
            ],
            out_specs=pl.BlockSpec((G, rows, 128), lambda i, s: (i, 0, 0)),
            scratch_shapes=[
                pltpu.VMEM((9 * pool + 8, 1, 128), f32),
                pltpu.VMEM((G * 256, 1, 128), f32),
                pltpu.VMEM((2, CH, 128), bf16),
                pltpu.VMEM((G, 128, 128), f32),
                pltpu.VMEM((G, 128, 128), f32),
                pltpu.SemaphoreType.DMA((2,)),
            ],
        ),
        out_shape=jax.ShapeDtypeStruct(state.shape, bf16),
        compiler_params=pltpu.CompilerParams(vmem_limit_bytes=56 * 1024 * 1024, dimension_semantics=("arbitrary",)),
        cost_estimate=pl.CostEstimate(flops=int(64*1.2e9), bytes_accessed=24_000_000, transcendentals=0),
        name="analyse_patches",
    )(idx, *tiles, vals, upd, state)


def shift_tile(value, axis, step, wrap):
    devices = lax.axis_size(axis)
    pairs = [(i, (i + step) % devices) for i in range(devices) if wrap or 0 <= i + step < devices]
    return lax.ppermute(value, axis, pairs)


def around(value):
    row = [shift_tile(value, "lon", 1, True), value, shift_tile(value, "lon", -1, True)]
    before = [shift_tile(tile, "lat", 1, False) for tile in row]
    after = [shift_tile(tile, "lat", -1, False) for tile in row]
    return before + row + after


def shards(state, ocean_mask, obs_pert, innovation, precision, obs_index, obs_count):
    members = obs_pert.shape[-1]
    pool = obs_pert.shape[2]
    patches, slots = obs_index.shape[2:]
    root_prec = jnp.sqrt(precision[0, 0])
    scaled = (root_prec[:, None] * obs_pert[0, 0].astype(f32)).astype(bf16)
    weighted = (root_prec * innovation[0, 0]).astype(bf16).reshape(pool // members, members)
    tiles = around(scaled)
    vals = jnp.stack(around(weighted)).reshape(-1)
    counts = obs_count[0, 0]
    picks = obs_index[0, 0]
    in_window = jnp.arange(slots, dtype=jnp.int32)[None, :] < counts[:, None]
    picked_vals = jnp.where(in_window, vals[picks].astype(f32), 0.0)
    places = jnp.where(in_window, picks, 9 * pool)
    updated = ((counts > 0)[:, None] & (ocean_mask[0, 0] > 0)).astype(f32)
    updated = jnp.broadcast_to(updated[:, :, None], updated.shape + (members,))
    columns = state.reshape(patches, -1, members)
    out = analyse_patches(places.reshape(-1), tiles, picked_vals, updated, columns)
    return out.reshape(state.shape)


def solution(mesh):
    placed = (
        P("lat", "lon", None, None, None, None),
        P("lat", "lon", None, None),
        P("lat", "lon", None, None),
        P("lat", "lon", None),
        P("lat", "lon", None),
        P("lat", "lon", None, None),
        P("lat", "lon", None),
    )
    return jax.shard_map(
        shards,
        mesh=mesh,
        in_specs=placed,
        out_specs=P("lat", "lon", None, None, None, None),
        check_vma=False,
    )
```

```python
import functools
import jax, jax.numpy as jnp
from jax import lax
from jax.sharding import PartitionSpec as P
from jax.experimental import pallas as pl
from jax.experimental.pallas import tpu as pltpu

SWEEPS = 8
f32, bf16 = jnp.float32, jnp.bfloat16

def wide(x):
    hi = x.astype(bf16)
    lo = (x - hi.astype(f32)).astype(bf16)
    return jnp.concatenate([hi, lo], axis=1)

def times(left, right):
    out = jnp.dot(left, jnp.concatenate([right, right], axis=0), preferred_element_type=f32)
    half = out.shape[1] // 2
    return out[:, :half] + out[:, half:]

def body(G, CH, AB, idx_ref, val_ref, *refs):
    tiles = refs[:9]
    upd_ref, state_ref, out_ref, table, picked, stage, acc, nref, tref, zref, wref, sem = refs[9:]
    step = pl.program_id(0)
    steps = pl.num_programs(0)
    members = 128
    lanes = idx_ref.shape[1]
    slots = picked.shape[1] // G
    per = slots // lanes
    pool = tiles[0].shape[0]
    inner = SWEEPS - 2

    def pick(group, buf, g, start, count):
        p = (group * G + g) * per
        base = pl.multiple_of(g * slots, slots)
        sums = [jnp.zeros((1, members), f32) for _ in range(4)]
        for u in range(start, start + count):
            i = idx_ref[p + u // lanes, u % lanes]
            row = table[pl.ds(i, 1), :]
            picked[buf, pl.ds(base + u, 1), :] = row
            sums[u % 4] = sums[u % 4] + row * val_ref[i]
        return (sums[0] + sums[1]) + (sums[2] + sums[3])

    def fetch(t):
        return pltpu.make_async_copy(tiles[t].at[pl.ds(0, pool)], stage.at[t], sem.at[t])

    @pl.when(step == (-1 if 't' in AB else 0))
    def _():
        for t in range(9):
            fetch(t).start()
        for t in range(9):
            fetch(t).wait()
            def convert(c, _):
                table[pl.ds(t * pool + c * CH, CH), :] = stage[t, pl.ds(c * CH, CH), :].astype(f32)
                return 0
            lax.fori_loop(0, pool // CH, convert, 0)
        table[pl.ds(9 * pool, 8)] = jnp.zeros((8, members), f32)

    @pl.when(step == 0)
    def _():
        def first(g, _):
            acc[0, g] = jnp.broadcast_to(pick(0, 0, g, 0, slots), (8, members))
            return 0
        lax.fori_loop(0, G, first, 0)

    now = lax.rem(step, 2)
    nxt = 1 - now
    group = jnp.minimum(step + 1, steps - 1)

    rows_i = lax.broadcasted_iota(jnp.int32, (members, members), 0)
    cols_i = lax.broadcasted_iota(jnp.int32, (members, members), 1)
    eye = (rows_i == cols_i).astype(f32)
    frob = []
    for g in range(G):
        rows = picked[now, pl.ds(g * slots, slots), :].astype(bf16)
        gram = lax.dot_general(rows, rows, (((0,), (0,)), ((), ())), preferred_element_type=f32)
        system = eye + gram * f32(1.0 / 127.0)
        fr = jnp.sqrt(jnp.sum(system * system, axis=(0, 1), keepdims=True))
        frob.append(fr)
        n = system * (-0.5 / fr)
        nref[g] = n
        zref[g] = 1.5 * eye + n
        wref[g] = wide(n)
    for g in range(G):
        nw = wref[g]
        tref[g] = 1.5 * nref[g] + times(nw, nw)
    for g in range(inner, G):
        acc[nxt, g] = jnp.broadcast_to(pick(group, nxt, g, 0, slots), (8, members))
    for g in range(G):
        t = tref[g]
        nref[g] = 1.5 * t + times(wide(t), wref[g])

    def sweep(k, _):
        total = jnp.zeros((1, members), f32)
        for g in range(G):
            n = nref[g]
            z = zref[g]
            nw = wide(n)
            wref[g] = nw
            R = times(jnp.concatenate([nw, wide(z)], axis=0), nw)
            tref[g] = 1.5 * n + R[:members]
            zref[g] = 1.5 * z + R[members:]
            if 'g' not in AB:
                total = total + pick(group, nxt, k, g * (slots // G), slots // G)
        acc[nxt, k] = jnp.broadcast_to(total, (8, members))
        for g in range(G):
            t = tref[g]
            nref[g] = 1.5 * t + times(wide(t), wref[g])
        return 0
    lax.fori_loop(0, 0 if 's' in AB else inner, sweep, 0)

    if 'e' not in AB:
      for g in range(G):
        z = zref[g]
        z = 1.5 * z + times(wide(z), wide(nref[g]))
        root = z / jnp.sqrt(frob[g] * f32(127.0))
        zref[g] = root
        wref[g] = wide(root)
      means = []
      for g in range(G):
        proj = acc[now, g]
        means.append(times(wide(proj), wref[g]))
      for g in range(G):
        means[g] = times(wide(means[g]), wref[g])
      for g in range(G):
        weights_t = (jnp.sqrt(f32(127.0)) * zref[g] + means[g][:1]).astype(bf16)
        values = state_ref[g].astype(f32)
        center = jnp.sum(values, axis=-1, keepdims=True) * f32(1.0 / members)
        spread = (values - center).astype(bf16)
        got = center + lax.dot_general(spread, weights_t, (((1,), (1,)), ((), ())), preferred_element_type=f32)
        n = values.shape[0]
        res = jnp.where(upd_ref[g][None] > 0, got.reshape(n // 8, 8, members), values.reshape(n // 8, 8, members))
        out_ref[g] = res.reshape(n, members).astype(bf16)

def analyse_patches(idx, vals, tiles, upd, state, G=8, CH=512, AB=''):
    N = state.shape[0]
    slots = idx.size // N
    idx = idx.reshape(-1, 128)
    pool = tiles[0].shape[0]
    rows = state.shape[1]
    return pl.pallas_call(
        functools.partial(body, G, CH, AB),
        grid_spec=pltpu.PrefetchScalarGridSpec(
            num_scalar_prefetch=2,
            grid=(N // G,),
            in_specs=[pl.BlockSpec(memory_space=pl.ANY)] * 9 + [
                pl.BlockSpec((G, 8, 128), lambda i, *s: (i, 0, 0)),
                pl.BlockSpec((G, rows, 128), lambda i, *s: (i, 0, 0)),
            ],
            out_specs=pl.BlockSpec((G, rows, 128), lambda i, *s: (i, 0, 0)),
            scratch_shapes=[
                pltpu.VMEM((9 * pool + 8, 128), f32),
                pltpu.VMEM((2, G * slots, 128), f32),
                pltpu.VMEM((9, pool, 128), bf16),
                pltpu.VMEM((2, G, 8, 128), f32),
                pltpu.VMEM((G, 128, 128), f32),
                pltpu.VMEM((G, 128, 128), f32),
                pltpu.VMEM((G, 128, 128), f32),
                pltpu.VMEM((G, 128, 256), bf16),
                pltpu.SemaphoreType.DMA((9,)),
            ],
        ),
        out_shape=jax.ShapeDtypeStruct(state.shape, bf16),
        compiler_params=pltpu.CompilerParams(vmem_limit_bytes=56 * 1024 * 1024, dimension_semantics=("arbitrary",)),
        cost_estimate=pl.CostEstimate(flops=int(64*1.2e9), bytes_accessed=24_000_000, transcendentals=0),
        name="analyse_patches",
    )(idx, vals, *tiles, upd, state)


MESH = pl.DeviceIdType.MESH
PIECES = 4


def halo_body(lats, lons, own, own_vals, zeros, *refs):
    outs = refs[:8]
    vals = refs[8]
    row_send, row_recv, val_send, val_recv, local = refs[9:]
    a, b = lax.axis_index("lat"), lax.axis_index("lon")
    pool = own.shape[0]
    size = pool // PIECES
    slots = {}
    for u in range(3):
        for v in range(3):
            if (u, v) != (1, 1):
                slots[u, v] = outs[len(slots)]

    def at(u, v):
        return (a + u, lax.rem(b + v + lons, lons))

    def rows(u, v, source, target, piece, number):
        return pltpu.make_async_remote_copy(
            src_ref=source.at[pl.ds(piece * size, size)],
            dst_ref=slots[target].at[pl.ds(piece * size, size)],
            send_sem=row_send.at[number, piece],
            recv_sem=row_recv.at[number, piece],
            device_id=at(u, v),
            device_id_type=MESH,
        )

    def place(u, v):
        return vals.at[pl.ds((3 * u + v) * pool, pool)]

    def numbers(u, v, source, target, number):
        return pltpu.make_async_remote_copy(
            src_ref=source,
            dst_ref=place(*target),
            send_sem=val_send.at[number],
            recv_sem=val_recv.at[number],
            device_id=at(u, v),
            device_id_type=MESH,
        )

    has_up, has_down = a > 0, a < lats - 1
    barrier = pltpu.get_barrier_semaphore()
    for v in (-1, 1):
        pl.semaphore_signal(barrier, inc=1, device_id=at(0, v), device_id_type=MESH)

    @pl.when(has_up)
    def _():
        pl.semaphore_signal(barrier, inc=1, device_id=at(-1, 0), device_id_type=MESH)

    @pl.when(has_down)
    def _():
        pl.semaphore_signal(barrier, inc=1, device_id=at(1, 0), device_id_type=MESH)

    pl.semaphore_wait(barrier, 2 + jnp.minimum(a, 1) + jnp.minimum(lats - 1 - a, 1))

    keep = [
        pltpu.make_async_copy(own_vals, place(1, 1), local.at[0]),
        pltpu.make_async_copy(zeros, vals.at[pl.ds(9 * pool, zeros.shape[0])], local.at[1]),
    ]
    for copy in keep:
        copy.start()

    sides = [(0, 1), (0, -1)]
    across = [rows(0, 1, own, (1, 0), p, 0) for p in range(PIECES)], [rows(0, -1, own, (1, 2), p, 1) for p in range(PIECES)]
    across_vals = [numbers(0, 1, own_vals, (1, 0), 0), numbers(0, -1, own_vals, (1, 2), 1)]
    source = [slots[1, 0], own, slots[1, 2]]
    source_vals = [place(1, 0), own_vals, place(1, 2)]
    down = [[rows(1, 0, source[w], (0, w), p, 2 + 2 * w) for p in range(PIECES)] for w in range(3)]
    up = [[rows(-1, 0, source[w], (2, w), p, 3 + 2 * w) for p in range(PIECES)] for w in range(3)]
    down_vals = [numbers(1, 0, source_vals[w], (0, w), 2 + 2 * w) for w in range(3)]
    up_vals = [numbers(-1, 0, source_vals[w], (2, w), 3 + 2 * w) for w in range(3)]

    for copy in across_vals:
        copy.start()
    for p in range(PIECES):
        across[0][p].start()
        across[1][p].start()

    def onward(copies_down, copies_up):
        @pl.when(has_down)
        def _():
            for copy in copies_down:
                copy.start()

        @pl.when(has_up)
        def _():
            for copy in copies_up:
                copy.start()

    onward([down_vals[1]] + down[1], [up_vals[1]] + up[1])
    across_vals[0].wait_recv()
    onward([down_vals[0]], [up_vals[0]])
    across_vals[1].wait_recv()
    onward([down_vals[2]], [up_vals[2]])
    for p in range(PIECES):
        for d in range(2):
            across[d][p].wait_recv()
            onward([down[2 * d][p]], [up[2 * d][p]])

    for copy in keep:
        copy.wait()
    for copy in across_vals + across[0] + across[1]:
        copy.wait_send()

    @pl.when(has_down)
    def _():
        for copy in down_vals + sum(down, []):
            copy.wait_send()
        for copy in up_vals + sum(up, []):
            copy.wait_recv()

    @pl.when(has_up)
    def _():
        for copy in up_vals + sum(up, []):
            copy.wait_send()
        for copy in down_vals + sum(down, []):
            copy.wait_recv()


def halo(own, own_vals):
    lats, lons = lax.axis_size("lat"), lax.axis_size("lon")
    pool, members = own.shape
    tail = jnp.zeros((1024,), f32)
    got = pl.pallas_call(
        functools.partial(halo_body, lats, lons),
        in_specs=[pl.BlockSpec(memory_space=pl.ANY)] * 3,
        out_specs=[pl.BlockSpec(memory_space=pl.ANY)] * 9,
        out_shape=[jax.ShapeDtypeStruct((pool, members), bf16)] * 8
        + [jax.ShapeDtypeStruct((9 * pool + 1024,), f32)],
        scratch_shapes=[
            pltpu.SemaphoreType.DMA((8, PIECES)),
            pltpu.SemaphoreType.DMA((8, PIECES)),
            pltpu.SemaphoreType.DMA((8,)),
            pltpu.SemaphoreType.DMA((8,)),
            pltpu.SemaphoreType.DMA((2,)),
        ],
        compiler_params=pltpu.CompilerParams(collective_id=0, has_side_effects=True),
        name="halo",
    )(own, own_vals, tail)
    return list(got[:4]) + [own] + list(got[4:8]), got[8]


def shards(state, ocean_mask, obs_pert, innovation, precision, obs_index, obs_count):
    members = obs_pert.shape[-1]
    pool = obs_pert.shape[2]
    patches, slots = obs_index.shape[2:]
    root_prec = jnp.sqrt(precision[0, 0])
    scaled = (root_prec[:, None] * obs_pert[0, 0].astype(f32)).astype(bf16)
    weighted = (root_prec * innovation[0, 0]).astype(bf16).astype(f32)
    tiles, vals = halo(scaled, weighted)
    counts = obs_count[0, 0]
    picks = obs_index[0, 0]
    in_window = jnp.arange(slots, dtype=jnp.int32)[None, :] < counts[:, None]
    places = jnp.where(in_window, picks, 9 * pool)
    updated = ((counts > 0)[:, None] & (ocean_mask[0, 0] > 0)).astype(f32)
    updated = jnp.broadcast_to(updated[:, :, None], updated.shape + (members,))
    columns = state.reshape(patches, -1, members)
    out = analyse_patches(places, vals, tiles, updated, columns)
    return out.reshape(state.shape)


def solution(mesh):
    placed = (
        P("lat", "lon", None, None, None, None),
        P("lat", "lon", None, None),
        P("lat", "lon", None, None),
        P("lat", "lon", None),
        P("lat", "lon", None),
        P("lat", "lon", None, None),
        P("lat", "lon", None),
    )
    return jax.shard_map(
        shards,
        mesh=mesh,
        in_specs=placed,
        out_specs=P("lat", "lon", None, None, None, None),
        check_vma=False,
    )
```

```python
import functools
import jax, jax.numpy as jnp
from jax import lax
from jax.sharding import PartitionSpec as P
from jax.experimental import pallas as pl
from jax.experimental.pallas import tpu as pltpu

SWEEPS = 8
f32, bf16 = jnp.float32, jnp.bfloat16
ROOT = 4.6128878647175444
SLOPE_A, SHIFT_A = (3 + ROOT) / 2, 3 * ROOT / 4
SLOPE_B, SHIFT_B = (6 - ROOT) / 2, 3 / ROOT

def wide(x):
    hi = x.astype(bf16)
    lo = (x - hi.astype(f32)).astype(bf16)
    return jnp.concatenate([hi, lo], axis=1)

def times(left, right):
    out = jnp.dot(left, jnp.concatenate([right, right], axis=0), preferred_element_type=f32)
    half = out.shape[1] // 2
    return out[:, :half] + out[:, half:]

def body(G, CH, AB, count_ref, mask_ref, idx_hbm, val_hbm, *refs):
    tiles = refs[:9]
    state_ref, out_ref, idx_ref, val_ref, table, picked, worth, diag, stage, acc, mref, tref, zref, wref, qref, sem, smem_sem = refs[9:]
    step = pl.program_id(0)
    steps = pl.num_programs(0)
    members = 128
    lanes = idx_ref.shape[1]
    slots = picked.shape[0] // G
    patches = steps * G
    pool = tiles[0].shape[0]

    def pick(group, g, start, count):
        p = group * G + g
        base = pl.multiple_of(g * slots, slots)
        for u in range(start, start + count):
            i = idx_ref[p + u // lanes * patches, u % lanes]
            picked[pl.ds(base + u, 1), :] = table[pl.ds(i, 1), :]
            worth[pl.ds(base + u, 1), :] = jnp.full((1, members), val_ref[i], f32)

    rows_i = lax.broadcasted_iota(jnp.int32, (members, members), 0)
    cols_i = lax.broadcasted_iota(jnp.int32, (members, members), 1)
    eye = (rows_i == cols_i).astype(f32)

    def fetch(t):
        return pltpu.make_async_copy(tiles[t].at[pl.ds(0, pool)], stage.at[t], sem.at[t])

    @pl.when(step == (-1 if 't' in AB else 0))
    def _():
        scalars = [pltpu.make_async_copy(idx_hbm, idx_ref, smem_sem.at[0]), pltpu.make_async_copy(val_hbm, val_ref, smem_sem.at[1])]
        for copy in scalars:
            copy.start()
        for t in range(9):
            fetch(t).start()
        for t in range(9):
            fetch(t).wait()
            def convert(c, _):
                table[pl.ds(t * pool + c * CH, CH), :] = stage[t, pl.ds(c * CH, CH), :].astype(f32)
                return 0
            lax.fori_loop(0, pool // CH, convert, 0)
        table[pl.ds(9 * pool, 8)] = jnp.zeros((8, members), f32)
        for copy in scalars:
            copy.wait()

    @pl.when(step == 0)
    def _():
        for j in range(2):
            diag[j] = eye * (SHIFT_A, SHIFT_B)[j]

        def first(g, _):
            pick(0, g, 0, slots)
            return 0
        lax.fori_loop(0, G, first, 0)

    group = jnp.minimum(step + 1, steps - 1)

    column = lax.broadcasted_iota(jnp.int32, (8, members), 0)

    def gather(patches, stage_no):
        count = len(patches) * slots // 4 // G
        def some(g):
            for u in range((stage_no * G + g) * count, (stage_no * G + g + 1) * count, 8):
                pick(group, patches[u // slots], u % slots, 8)
        return some

    def nothing(g):
        pass

    def square(some):
        for g in range(G):
            mw = wide(mref[g])
            wref[g] = mw
            tref[g] = times(mw, mw)
            some(g)

    def factor(some):
        for g in range(G):
            m, m2 = mref[g], tref[g]
            left = m2 - SLOPE_A * m + diag[0]
            right = m2 - SLOPE_B * m + diag[1]
            q = times(wide(left), wide(right))
            qref[g] = wide(q)
            if some is None:
                zref[g] = q
            else:
                some(g)

    def finish(some):
        for g in range(G):
            mref[g] = times(wide(tref[g]), qref[g])
            some(g)

    frob = []
    for g in range(G):
        rows = picked[pl.ds(g * slots, slots), :].astype(bf16)
        value = worth[pl.ds(g * slots, slots), :].astype(bf16)
        both = lax.dot_general(rows, jnp.concatenate([rows, value], axis=1), (((0,), (0,)), ((), ())), preferred_element_type=f32)
        acc[g] = both[:, members:].T[:8]
        system = eye + both[:, :members] * f32(1.0 / 127.0)
        fr = jnp.sqrt(jnp.sum(system * system, axis=(0, 1), keepdims=True))
        frob.append(fr)
        mref[g] = system * (0.5 / fr)
    square(nothing)
    factor(None)
    for g in range(G):
        tref[g] = times(wref[g], qref[g])
    finish(nothing)

    def sweep(k, _):
        square(gather([3 * k, 3 * k + 1, 3 * k + 2], 0))
        factor(gather([3 * k, 3 * k + 1, 3 * k + 2], 1))
        some = gather([3 * k, 3 * k + 1, 3 * k + 2], 2)
        for g in range(G):
            out = times(jnp.concatenate([wref[g], wide(zref[g])], axis=0), qref[g])
            tref[g] = out[:members]
            zref[g] = out[members:]
            some(g)
        finish(gather([3 * k, 3 * k + 1, 3 * k + 2], 3))
        return 0
    lax.fori_loop(0, 0 if 's' in AB else SWEEPS // 2 - 2, sweep, 0)

    square(gather([6, 7], 0))
    factor(gather([6, 7], 1))
    some = gather([6, 7], 2)
    for g in range(G):
        root = times(wide(zref[g]), qref[g]) * (1.0 / jnp.sqrt(frob[g] * f32(127.0)))
        zref[g] = root
        wref[g] = wide(root)
        some(g)
    some = gather([6, 7], 3)
    means = []
    for g in range(G):
        means.append(times(wide(acc[g]), wref[g]))
        some(g)
    for g in range(G):
        means[g] = times(wide(means[g]), wref[g])
    for g in range(G):
        weights_t = (jnp.sqrt(f32(127.0)) * zref[g] + means[g][:1]).astype(bf16)
        patch = step * G + g
        seen = count_ref[patch] > 0
        land = jnp.zeros((8, members), jnp.int32)
        for c in range(8):
            land = jnp.where(column == c, jnp.where(seen, mask_ref[patch, c], 0), land)
        values = state_ref[g].astype(f32)
        center = jnp.sum(values, axis=-1, keepdims=True) * f32(1.0 / members)
        spread = (values - center).astype(bf16)
        got = center + lax.dot_general(spread, weights_t, (((1,), (1,)), ((), ())), preferred_element_type=f32)
        n = values.shape[0]
        res = jnp.where(land[None] > 0, got.reshape(n // 8, 8, members), values.reshape(n // 8, 8, members))
        out_ref[g] = res.reshape(n, members).astype(bf16)

def analyse_patches(idx, vals, counts, mask, tiles, state, G=8, CH=512, AB=''):
    N = state.shape[0]
    slots = idx.size // N
    pool = tiles[0].shape[0]
    rows = state.shape[1]
    return pl.pallas_call(
        functools.partial(body, G, CH, AB),
        grid_spec=pltpu.PrefetchScalarGridSpec(
            num_scalar_prefetch=2,
            grid=(N // G,),
            in_specs=[pl.BlockSpec(memory_space=pl.ANY)] * 11 + [
                pl.BlockSpec((G, rows, 128), lambda i, *s: (i, 0, 0)),
            ],
            out_specs=pl.BlockSpec((G, rows, 128), lambda i, *s: (i, 0, 0)),
            scratch_shapes=[
                pltpu.SMEM(idx.shape, jnp.int32),
                pltpu.SMEM(vals.shape, f32),
                pltpu.VMEM((9 * pool + 8, 128), f32),
                pltpu.VMEM((G * slots, 128), f32),
                pltpu.VMEM((G * slots, 128), f32),
                pltpu.VMEM((2, 128, 128), f32),
                pltpu.VMEM((9, pool, 128), bf16),
                pltpu.VMEM((G, 8, 128), f32),
                pltpu.VMEM((G, 128, 128), f32),
                pltpu.VMEM((G, 128, 128), f32),
                pltpu.VMEM((G, 128, 128), f32),
                pltpu.VMEM((G, 128, 256), bf16),
                pltpu.VMEM((G, 128, 256), bf16),
                pltpu.SemaphoreType.DMA((9,)),
                pltpu.SemaphoreType.DMA((2,)),
            ],
        ),
        out_shape=jax.ShapeDtypeStruct(state.shape, bf16),
        compiler_params=pltpu.CompilerParams(vmem_limit_bytes=56 * 1024 * 1024, dimension_semantics=("arbitrary",)),
        cost_estimate=pl.CostEstimate(flops=int(64*1.2e9), bytes_accessed=24_000_000, transcendentals=0),
        name="analyse_patches",
    )(counts, mask, idx, vals, *tiles, state)


MESH = pl.DeviceIdType.MESH
PIECES = 4
ASIDE = 1


def halo_body(lats, lons, pert, innov, prec, picks, counts, *refs):
    outs = refs[:8]
    own_out, vals, places = refs[8:11]
    own, own_vals, zeros, row_send, row_recv, val_send, val_recv, side_send, local = refs[11:]
    a, b = lax.axis_index("lat"), lax.axis_index("lon")
    pool, members = own.shape
    size = pool // PIECES
    lines = pool // members
    slots = {}
    for u in range(3):
        for v in range(3):
            if (u, v) != (1, 1):
                slots[u, v] = outs[len(slots)]

    def at(u, v):
        return (a + u, lax.rem(b + v + lons, lons))

    def rows(u, v, source, target, piece, number, send=None):
        return pltpu.make_async_remote_copy(
            src_ref=source.at[pl.ds(piece * size, size)],
            dst_ref=slots[target].at[pl.ds(piece * size, size)],
            send_sem=row_send.at[number, piece] if send is None else side_send.at[send, piece],
            recv_sem=row_recv.at[number, piece],
            device_id=at(u, v),
            device_id_type=MESH,
        )

    def place(u, v):
        return vals.at[pl.ds((3 * u + v) * lines, lines)]

    def numbers(u, v, source, target, number):
        return pltpu.make_async_remote_copy(
            src_ref=source,
            dst_ref=place(*target),
            send_sem=val_send.at[number],
            recv_sem=val_recv.at[number],
            device_id=at(u, v),
            device_id_type=MESH,
        )

    has_up, has_down = a > 0, a < lats - 1
    even = lax.rem(a, 2) == 0
    barrier = pltpu.get_barrier_semaphore()
    for v in (-1, 1):
        pl.semaphore_signal(barrier, inc=1, device_id=at(0, v), device_id_type=MESH)

    @pl.when(has_up)
    def _():
        pl.semaphore_signal(barrier, inc=1, device_id=at(-1, 0), device_id_type=MESH)

    @pl.when(has_down)
    def _():
        pl.semaphore_signal(barrier, inc=1, device_id=at(1, 0), device_id_type=MESH)

    across = [[rows(0, 1, own, (1, 0), p, 0) for p in range(PIECES)], [rows(0, -1, own, (1, 2), p, 1) for p in range(PIECES)]]
    across_vals = [numbers(0, 1, own_vals, (1, 0), 0), numbers(0, -1, own_vals, (1, 2), 1)]
    source = [slots[1, 0], own, slots[1, 2]]
    source_vals = [place(1, 0), own_vals, place(1, 2)]
    down = [[rows(1, 0, source[w], (0, w), p, 2 + 2 * w) for p in range(PIECES)] for w in range(3)]
    up = [[rows(-1, 0, source[w], (2, w), p, 3 + 2 * w) for p in range(PIECES)] for w in range(3)]
    down_vals = [numbers(1, 0, source_vals[w], (0, w), 2 + 2 * w) for w in range(3)]
    up_vals = [numbers(-1, 0, source_vals[w], (2, w), 3 + 2 * w) for w in range(3)]
    last = range(PIECES - ASIDE, PIECES)
    side_up = [rows(0, 1, slots[0, 1], (0, 0), p, 2, 0) for p in last] + [rows(0, -1, slots[0, 1], (0, 2), p, 6, 1) for p in last]
    side_down = [rows(0, 1, slots[2, 1], (2, 0), p, 3, 0) for p in last] + [rows(0, -1, slots[2, 1], (2, 2), p, 7, 1) for p in last]

    def onward(copies_down, copies_up, aside=False):
        @pl.when(has_down & even if aside else has_down)
        def _():
            for copy in copies_down:
                copy.start()

        @pl.when(has_up & jnp.logical_not(even) if aside else has_up)
        def _():
            for copy in copies_up:
                copy.start()

    root = jnp.sqrt(prec[...])
    own_vals[...] = (root * innov[...]).astype(bf16).astype(f32)
    zeros[...] = jnp.zeros_like(zeros)
    turned = jnp.concatenate([root] * (members // lines), axis=0).T
    for p in range(PIECES):
        for r in range(p * lines // PIECES, (p + 1) * lines // PIECES):
            here = pl.ds(r * members, members)
            own[here, :] = (turned[:, r : r + 1] * pert[here, :].astype(f32)).astype(bf16)
        if p == 0:
            pl.semaphore_wait(barrier, 2 + jnp.minimum(a, 1) + jnp.minimum(lats - 1 - a, 1))
        across[0][p].start()
        across[1][p].start()
        onward([down[1][p]], [up[1][p]])
        if p == 0:
            for copy in across_vals:
                copy.start()
            onward([down_vals[1]], [up_vals[1]])
    keep = [
        pltpu.make_async_copy(own, own_out, local.at[0]),
        pltpu.make_async_copy(own_vals, place(1, 1), local.at[1]),
        pltpu.make_async_copy(zeros, vals.at[pl.ds(9 * lines, zeros.shape[0])], local.at[2]),
    ]
    for copy in keep:
        copy.start()

    patches = counts.shape[1]
    line = lax.broadcasted_iota(jnp.int32, (patches, patches), 0)
    same = line == lax.broadcasted_iota(jnp.int32, (patches, patches), 1)
    spread_counts = jnp.broadcast_to(counts[...].astype(f32), (patches, patches))
    limit = jnp.sum(jnp.where(same, spread_counts, 0.0), axis=1, keepdims=True)
    slot = lax.broadcasted_iota(jnp.int32, (patches, members), 1).astype(f32)
    for h in range(picks.shape[1] // members):
        seen = slot + h * members < limit
        places[pl.ds(h * patches, patches), :] = jnp.where(seen, picks[:, h * members : (h + 1) * members], 9 * pool)

    across_vals[0].wait_recv()
    onward([down_vals[0]], [up_vals[0]])
    across_vals[1].wait_recv()
    onward([down_vals[2]], [up_vals[2]])
    for p in range(PIECES):
        if p == PIECES - ASIDE:

            @pl.when(even & has_up)
            def _():
                for q in last:
                    down[1][q].wait_recv()
                for copy in side_up:
                    copy.start()

            @pl.when(jnp.logical_not(even) & has_down)
            def _():
                for q in last:
                    up[1][q].wait_recv()
                for copy in side_down:
                    copy.start()

        for d in range(2):
            across[d][p].wait_recv()
            onward([down[2 * d][p]], [up[2 * d][p]], p in last)

    for copy in keep:
        copy.wait()
    for copy in across_vals + across[0] + across[1]:
        copy.wait_send()

    def corners(copies, pieces):
        return [copies[w][p] for w in (0, 2) for p in pieces]

    first = range(PIECES - ASIDE)

    @pl.when(has_down)
    def _():
        for copy in down_vals + down[1] + corners(down, first):
            copy.wait_send()
        for copy in up_vals + up[1][: PIECES - ASIDE] + corners(up, range(PIECES)):
            copy.wait_recv()

    @pl.when(has_up)
    def _():
        for copy in up_vals + up[1] + corners(up, first):
            copy.wait_send()
        for copy in down_vals + down[1][: PIECES - ASIDE] + corners(down, range(PIECES)):
            copy.wait_recv()

    @pl.when(has_down & even)
    def _():
        for copy in corners(down, last):
            copy.wait_send()
        for copy in up[1][PIECES - ASIDE :]:
            copy.wait_recv()

    @pl.when(has_up & jnp.logical_not(even))
    def _():
        for copy in corners(up, last):
            copy.wait_send()
        for copy in down[1][PIECES - ASIDE :]:
            copy.wait_recv()

    @pl.when(has_up & even)
    def _():
        for copy in side_up:
            copy.wait_send()

    @pl.when(has_down & jnp.logical_not(even))
    def _():
        for copy in side_down:
            copy.wait_send()


def halo(pert, innov, prec, picks, counts):
    lats, lons = lax.axis_size("lat"), lax.axis_size("lon")
    pool, members = pert.shape
    lines = pool // members
    vmem = pl.BlockSpec(memory_space=pltpu.VMEM)
    anywhere = pl.BlockSpec(memory_space=pl.ANY)
    got = pl.pallas_call(
        functools.partial(halo_body, lats, lons),
        in_specs=[vmem] * 5,
        out_specs=[anywhere] * 10 + [vmem],
        out_shape=[jax.ShapeDtypeStruct((pool, members), bf16)] * 9
        + [
            jax.ShapeDtypeStruct((9 * lines + 8, members), f32),
            jax.ShapeDtypeStruct((picks.size // members, members), jnp.int32),
        ],
        scratch_shapes=[
            pltpu.VMEM((pool, members), bf16),
            pltpu.VMEM((lines, members), f32),
            pltpu.VMEM((8, members), f32),
            pltpu.SemaphoreType.DMA((8, PIECES)),
            pltpu.SemaphoreType.DMA((8, PIECES)),
            pltpu.SemaphoreType.DMA((8,)),
            pltpu.SemaphoreType.DMA((8,)),
            pltpu.SemaphoreType.DMA((2, PIECES)),
            pltpu.SemaphoreType.DMA((3,)),
        ],
        compiler_params=pltpu.CompilerParams(collective_id=0, has_side_effects=True),
        name="halo",
    )(pert, innov, prec, picks, counts)
    return list(got[:4]) + [got[8]] + list(got[4:8]), got[9], got[10]


def shards(state, ocean_mask, obs_pert, innovation, precision, obs_index, obs_count):
    pool, members = obs_pert.shape[2:]
    patches = obs_index.shape[2]
    lines = (pool // members, members)
    tiles, vals, places = halo(
        obs_pert[0, 0], innovation.reshape(lines), precision.reshape(lines), obs_index[0, 0], obs_count[0]
    )
    columns = state.reshape(patches, -1, members)
    out = analyse_patches(places, vals.reshape(-1), obs_count[0, 0], ocean_mask[0, 0], tiles, columns)
    return out.reshape(state.shape)


def solution(mesh):
    placed = (
        P("lat", "lon", None, None, None, None),
        P("lat", "lon", None, None),
        P("lat", "lon", None, None),
        P("lat", "lon", None),
        P("lat", "lon", None),
        P("lat", "lon", None, None),
        P("lat", "lon", None),
    )
    return jax.shard_map(
        shards,
        mesh=mesh,
        in_specs=placed,
        out_specs=P("lat", "lon", None, None, None, None),
        check_vma=False,
    )
```

```python
import functools
import jax, jax.numpy as jnp
from jax import lax
from jax.sharding import PartitionSpec as P
from jax.experimental import pallas as pl
from jax.experimental.pallas import tpu as pltpu

SWEEPS = 8
f32, bf16 = jnp.float32, jnp.bfloat16
ROOT = 4.6128878647175444
SLOPE_A, SHIFT_A = (3 + ROOT) / 2, 3 * ROOT / 4
SLOPE_B, SHIFT_B = (6 - ROOT) / 2, 3 / ROOT

def wide(x):
    hi = x.astype(bf16)
    lo = (x - hi.astype(f32)).astype(bf16)
    return jnp.concatenate([hi, lo], axis=1)

def times(left, right):
    out = jnp.dot(left, jnp.concatenate([right, right], axis=0), preferred_element_type=f32)
    half = out.shape[1] // 2
    return out[:, :half] + out[:, half:]

def body(G, CH, AB, count_ref, mask_ref, idx_hbm, val_hbm, *refs):
    tiles = refs[:9]
    state_ref, out_ref, idx_ref, val_ref, table, picked, worth, diag, stage, acc, mref, tref, zref, wref, qref, sem, smem_sem = refs[9:]
    step = pl.program_id(0)
    steps = pl.num_programs(0)
    members = 128
    lanes = idx_ref.shape[1]
    slots = picked.shape[0] // G
    patches = steps * G
    pool = tiles[0].shape[0]

    def pick(g, start, count):
        for u in range(start, start + count):
            i = idx_ref[g + u // lanes * G, u % lanes]
            picked[pl.ds(g * slots + u, 1), :] = table[pl.ds(i, 1), :]
            worth[pl.ds(g * slots + u, 1), :] = jnp.full((1, members), val_ref[i], f32)

    def list_of(group):
        return [
            pltpu.make_async_copy(idx_hbm.at[pl.ds(h * patches + group * G, G)], idx_ref.at[pl.ds(h * G, G)], smem_sem.at[h])
            for h in range(slots // lanes)
        ]

    rows_i = lax.broadcasted_iota(jnp.int32, (members, members), 0)
    cols_i = lax.broadcasted_iota(jnp.int32, (members, members), 1)
    eye = (rows_i == cols_i).astype(f32)

    def fetch(t):
        return pltpu.make_async_copy(tiles[t].at[pl.ds(0, pool)], stage.at[t], sem.at[t])

    @pl.when(step == (-1 if 't' in AB else 0))
    def _():
        scalars = list_of(0) + [pltpu.make_async_copy(val_hbm, val_ref, smem_sem.at[slots // lanes])]
        for copy in scalars:
            copy.start()
        for t in range(9):
            fetch(t).start()
        for t in range(9):
            fetch(t).wait()
            def convert(c, _):
                table[pl.ds(t * pool + c * CH, CH), :] = stage[t, pl.ds(c * CH, CH), :].astype(f32)
                return 0
            lax.fori_loop(0, pool // CH, convert, 0)
        table[pl.ds(9 * pool, 8)] = jnp.zeros((8, members), f32)
        for copy in scalars:
            copy.wait()

    @pl.when(step == 0)
    def _():
        for j in range(2):
            diag[j] = eye * (SHIFT_A, SHIFT_B)[j]

        for g in range(G):
            pick(g, 0, slots)

    following = list_of(jnp.minimum(step + 1, steps - 1))
    for copy in following:
        copy.start()

    column = lax.broadcasted_iota(jnp.int32, (8, members), 0)

    def gather(patches, stage_no):
        count = len(patches) * slots // 4 // G
        def some(g):
            for u in range((stage_no * G + g) * count, (stage_no * G + g + 1) * count, 8):
                pick(patches[u // slots], u % slots, 8)
        return some

    def nothing(g):
        pass

    def square(some):
        for g in range(G):
            mw = wide(mref[g])
            wref[g] = mw
            tref[g] = times(mw, mw)
            some(g)

    def factor(some):
        for g in range(G):
            m, m2 = mref[g], tref[g]
            left = m2 - SLOPE_A * m + diag[0]
            right = m2 - SLOPE_B * m + diag[1]
            q = times(wide(left), wide(right))
            qref[g] = wide(q)
            if some is None:
                zref[g] = q
            else:
                some(g)

    def finish(some):
        for g in range(G):
            mref[g] = times(wide(tref[g]), qref[g])
            some(g)

    frob = []
    for g in range(G):
        chosen = picked[pl.ds(g * slots, slots), :]
        product = (chosen * worth[pl.ds(g * slots, slots), :]).reshape(slots // 8, 8, members)
        acc[g] = jnp.broadcast_to(jnp.sum(jnp.sum(product, axis=0), axis=0, keepdims=True), (8, members))
        rows = chosen.astype(bf16)
        gram = lax.dot_general(rows, rows, (((0,), (0,)), ((), ())), preferred_element_type=f32)
        system = eye + gram * f32(1.0 / 127.0)
        fr = jnp.sqrt(jnp.sum(system * system, axis=(0, 1), keepdims=True))
        frob.append(fr)
        mref[g] = system * (0.5 / fr)
    square(nothing)
    factor(None)
    for g in range(G):
        tref[g] = times(wref[g], qref[g])
    finish(nothing)

    for copy in following:
        copy.wait()

    def sweep(chosen):
        square(gather(chosen, 0))
        factor(gather(chosen, 1))
        some = gather(chosen, 2)
        for g in range(G):
            out = times(jnp.concatenate([wref[g], wide(zref[g])], axis=0), qref[g])
            tref[g] = out[:members]
            zref[g] = out[members:]
            some(g)
        finish(gather(chosen, 3))

    sweep([0, 1, 2])
    sweep([3, 4, 5])
    square(gather([6, 7], 0))
    factor(gather([6, 7], 1))
    some = gather([6, 7], 2)
    for g in range(G):
        root = times(wide(zref[g]), qref[g]) * (1.0 / jnp.sqrt(frob[g] * f32(127.0)))
        zref[g] = root
        wref[g] = wide(root)
        some(g)
    some = gather([6, 7], 3)
    means = []
    for g in range(G):
        means.append(times(wide(acc[g]), wref[g]))
        some(g)
    for g in range(G):
        means[g] = times(wide(means[g]), wref[g])
    for g in range(G):
        weights_t = (jnp.sqrt(f32(127.0)) * zref[g] + means[g][:1]).astype(bf16)
        patch = step * G + g
        seen = count_ref[patch] > 0
        land = jnp.zeros((8, members), jnp.int32)
        for c in range(8):
            land = jnp.where(column == c, jnp.where(seen, mask_ref[patch, c], 0), land)
        values = state_ref[g].astype(f32)
        center = jnp.sum(values, axis=-1, keepdims=True) * f32(1.0 / members)
        spread = (values - center).astype(bf16)
        got = center + lax.dot_general(spread, weights_t, (((1,), (1,)), ((), ())), preferred_element_type=f32)
        n = values.shape[0]
        res = jnp.where(land[None] > 0, got.reshape(n // 8, 8, members), values.reshape(n // 8, 8, members))
        out_ref[g] = res.reshape(n, members).astype(bf16)

def analyse_patches(idx, vals, counts, mask, tiles, state, G=8, CH=512, AB=''):
    N = state.shape[0]
    slots = idx.size // N
    pool = tiles[0].shape[0]
    rows = state.shape[1]
    return pl.pallas_call(
        functools.partial(body, G, CH, AB),
        grid_spec=pltpu.PrefetchScalarGridSpec(
            num_scalar_prefetch=2,
            grid=(N // G,),
            in_specs=[pl.BlockSpec(memory_space=pl.ANY)] * 11 + [
                pl.BlockSpec((G, rows, 128), lambda i, *s: (i, 0, 0)),
            ],
            out_specs=pl.BlockSpec((G, rows, 128), lambda i, *s: (i, 0, 0)),
            scratch_shapes=[
                pltpu.SMEM((G * slots // 128, 128), jnp.int32),
                pltpu.SMEM(vals.shape, f32),
                pltpu.VMEM((9 * pool + 8, 128), f32),
                pltpu.VMEM((G * slots, 128), f32),
                pltpu.VMEM((G * slots, 128), f32),
                pltpu.VMEM((2, 128, 128), f32),
                pltpu.VMEM((9, pool, 128), bf16),
                pltpu.VMEM((G, 8, 128), f32),
                pltpu.VMEM((G, 128, 128), f32),
                pltpu.VMEM((G, 128, 128), f32),
                pltpu.VMEM((G, 128, 128), f32),
                pltpu.VMEM((G, 128, 256), bf16),
                pltpu.VMEM((G, 128, 256), bf16),
                pltpu.SemaphoreType.DMA((9,)),
                pltpu.SemaphoreType.DMA((slots // 128 + 1,)),
            ],
        ),
        out_shape=jax.ShapeDtypeStruct(state.shape, bf16),
        compiler_params=pltpu.CompilerParams(vmem_limit_bytes=56 * 1024 * 1024, dimension_semantics=("arbitrary",)),
        cost_estimate=pl.CostEstimate(flops=int(64*1.2e9), bytes_accessed=24_000_000, transcendentals=0),
        name="analyse_patches",
    )(counts, mask, idx, vals, *tiles, state)


MESH = pl.DeviceIdType.MESH
PIECES = 4
ASIDE = 1


def halo_body(lats, lons, pert, innov, prec, picks, counts, *refs):
    outs = refs[:8]
    own_out, vals, places = refs[8:11]
    own, own_vals, zeros, row_send, row_recv, val_send, val_recv, side_send, local = refs[11:]
    a, b = lax.axis_index("lat"), lax.axis_index("lon")
    pool, members = own.shape
    size = pool // PIECES
    lines = pool // members
    slots = {}
    for u in range(3):
        for v in range(3):
            if (u, v) != (1, 1):
                slots[u, v] = outs[len(slots)]

    def at(u, v):
        return (a + u, lax.rem(b + v + lons, lons))

    def rows(u, v, source, target, piece, number, send=None):
        return pltpu.make_async_remote_copy(
            src_ref=source.at[pl.ds(piece * size, size)],
            dst_ref=slots[target].at[pl.ds(piece * size, size)],
            send_sem=row_send.at[number, piece] if send is None else side_send.at[send, piece],
            recv_sem=row_recv.at[number, piece],
            device_id=at(u, v),
            device_id_type=MESH,
        )

    def place(u, v):
        return vals.at[pl.ds((3 * u + v) * lines, lines)]

    def numbers(u, v, source, target, number):
        return pltpu.make_async_remote_copy(
            src_ref=source,
            dst_ref=place(*target),
            send_sem=val_send.at[number],
            recv_sem=val_recv.at[number],
            device_id=at(u, v),
            device_id_type=MESH,
        )

    has_up, has_down = a > 0, a < lats - 1
    even = lax.rem(a, 2) == 0
    barrier = pltpu.get_barrier_semaphore()
    for v in (-1, 1):
        pl.semaphore_signal(barrier, inc=1, device_id=at(0, v), device_id_type=MESH)

    @pl.when(has_up)
    def _():
        pl.semaphore_signal(barrier, inc=1, device_id=at(-1, 0), device_id_type=MESH)

    @pl.when(has_down)
    def _():
        pl.semaphore_signal(barrier, inc=1, device_id=at(1, 0), device_id_type=MESH)

    across = [[rows(0, 1, own, (1, 0), p, 0) for p in range(PIECES)], [rows(0, -1, own, (1, 2), p, 1) for p in range(PIECES)]]
    across_vals = [numbers(0, 1, own_vals, (1, 0), 0), numbers(0, -1, own_vals, (1, 2), 1)]
    source = [slots[1, 0], own, slots[1, 2]]
    source_vals = [place(1, 0), own_vals, place(1, 2)]
    down = [[rows(1, 0, source[w], (0, w), p, 2 + 2 * w) for p in range(PIECES)] for w in range(3)]
    up = [[rows(-1, 0, source[w], (2, w), p, 3 + 2 * w) for p in range(PIECES)] for w in range(3)]
    down_vals = [numbers(1, 0, source_vals[w], (0, w), 2 + 2 * w) for w in range(3)]
    up_vals = [numbers(-1, 0, source_vals[w], (2, w), 3 + 2 * w) for w in range(3)]
    last = range(PIECES - ASIDE, PIECES)
    side_up = [rows(0, 1, slots[0, 1], (0, 0), p, 2, 0) for p in last] + [rows(0, -1, slots[0, 1], (0, 2), p, 6, 1) for p in last]
    side_down = [rows(0, 1, slots[2, 1], (2, 0), p, 3, 0) for p in last] + [rows(0, -1, slots[2, 1], (2, 2), p, 7, 1) for p in last]

    def onward(copies_down, copies_up, aside=False):
        @pl.when(has_down & even if aside else has_down)
        def _():
            for copy in copies_down:
                copy.start()

        @pl.when(has_up & jnp.logical_not(even) if aside else has_up)
        def _():
            for copy in copies_up:
                copy.start()

    root = jnp.sqrt(prec[...])
    own_vals[...] = (root * innov[...]).astype(bf16).astype(f32)
    zeros[...] = jnp.zeros_like(zeros)
    turned = jnp.concatenate([root] * (members // lines), axis=0).T
    for p in range(PIECES):
        for r in range(p * lines // PIECES, (p + 1) * lines // PIECES):
            here = pl.ds(r * members, members)
            own[here, :] = (turned[:, r : r + 1] * pert[here, :].astype(f32)).astype(bf16)
        if p == 0:
            pl.semaphore_wait(barrier, 2 + jnp.minimum(a, 1) + jnp.minimum(lats - 1 - a, 1))
        across[0][p].start()
        across[1][p].start()
        onward([down[1][p]], [up[1][p]])
        if p == 0:
            for copy in across_vals:
                copy.start()
            onward([down_vals[1]], [up_vals[1]])
    keep = [
        pltpu.make_async_copy(own, own_out, local.at[0]),
        pltpu.make_async_copy(own_vals, place(1, 1), local.at[1]),
        pltpu.make_async_copy(zeros, vals.at[pl.ds(9 * lines, zeros.shape[0])], local.at[2]),
    ]
    for copy in keep:
        copy.start()

    patches = counts.shape[1]
    line = lax.broadcasted_iota(jnp.int32, (patches, patches), 0)
    same = line == lax.broadcasted_iota(jnp.int32, (patches, patches), 1)
    spread_counts = jnp.broadcast_to(counts[...].astype(f32), (patches, patches))
    limit = jnp.sum(jnp.where(same, spread_counts, 0.0), axis=1, keepdims=True)
    slot = lax.broadcasted_iota(jnp.int32, (patches, members), 1).astype(f32)
    for h in range(picks.shape[1] // members):
        seen = slot + h * members < limit
        places[pl.ds(h * patches, patches), :] = jnp.where(seen, picks[:, h * members : (h + 1) * members], 9 * pool)

    across_vals[0].wait_recv()
    onward([down_vals[0]], [up_vals[0]])
    across_vals[1].wait_recv()
    onward([down_vals[2]], [up_vals[2]])
    for p in range(PIECES):
        if p == PIECES - ASIDE:

            @pl.when(even & has_up)
            def _():
                for q in last:
                    down[1][q].wait_recv()
                for copy in side_up:
                    copy.start()

            @pl.when(jnp.logical_not(even) & has_down)
            def _():
                for q in last:
                    up[1][q].wait_recv()
                for copy in side_down:
                    copy.start()

        for d in range(2):
            across[d][p].wait_recv()
            onward([down[2 * d][p]], [up[2 * d][p]], p in last)

    for copy in keep:
        copy.wait()
    for copy in across_vals + across[0] + across[1]:
        copy.wait_send()

    def corners(copies, pieces):
        return [copies[w][p] for w in (0, 2) for p in pieces]

    first = range(PIECES - ASIDE)

    @pl.when(has_down)
    def _():
        for copy in down_vals + down[1] + corners(down, first):
            copy.wait_send()
        for copy in up_vals + up[1][: PIECES - ASIDE] + corners(up, range(PIECES)):
            copy.wait_recv()

    @pl.when(has_up)
    def _():
        for copy in up_vals + up[1] + corners(up, first):
            copy.wait_send()
        for copy in down_vals + down[1][: PIECES - ASIDE] + corners(down, range(PIECES)):
            copy.wait_recv()

    @pl.when(has_down & even)
    def _():
        for copy in corners(down, last):
            copy.wait_send()
        for copy in up[1][PIECES - ASIDE :]:
            copy.wait_recv()

    @pl.when(has_up & jnp.logical_not(even))
    def _():
        for copy in corners(up, last):
            copy.wait_send()
        for copy in down[1][PIECES - ASIDE :]:
            copy.wait_recv()

    @pl.when(has_up & even)
    def _():
        for copy in side_up:
            copy.wait_send()

    @pl.when(has_down & jnp.logical_not(even))
    def _():
        for copy in side_down:
            copy.wait_send()


def halo(pert, innov, prec, picks, counts):
    lats, lons = lax.axis_size("lat"), lax.axis_size("lon")
    pool, members = pert.shape
    lines = pool // members
    vmem = pl.BlockSpec(memory_space=pltpu.VMEM)
    anywhere = pl.BlockSpec(memory_space=pl.ANY)
    got = pl.pallas_call(
        functools.partial(halo_body, lats, lons),
        in_specs=[vmem] * 5,
        out_specs=[anywhere] * 10 + [vmem],
        out_shape=[jax.ShapeDtypeStruct((pool, members), bf16)] * 9
        + [
            jax.ShapeDtypeStruct((9 * lines + 8, members), f32),
            jax.ShapeDtypeStruct((picks.size // members, members), jnp.int32),
        ],
        scratch_shapes=[
            pltpu.VMEM((pool, members), bf16),
            pltpu.VMEM((lines, members), f32),
            pltpu.VMEM((8, members), f32),
            pltpu.SemaphoreType.DMA((8, PIECES)),
            pltpu.SemaphoreType.DMA((8, PIECES)),
            pltpu.SemaphoreType.DMA((8,)),
            pltpu.SemaphoreType.DMA((8,)),
            pltpu.SemaphoreType.DMA((2, PIECES)),
            pltpu.SemaphoreType.DMA((3,)),
        ],
        compiler_params=pltpu.CompilerParams(collective_id=0, has_side_effects=True),
        name="halo",
    )(pert, innov, prec, picks, counts)
    return list(got[:4]) + [got[8]] + list(got[4:8]), got[9], got[10]


def shards(state, ocean_mask, obs_pert, innovation, precision, obs_index, obs_count):
    pool, members = obs_pert.shape[2:]
    patches = obs_index.shape[2]
    lines = (pool // members, members)
    tiles, vals, places = halo(
        obs_pert[0, 0], innovation.reshape(lines), precision.reshape(lines), obs_index[0, 0], obs_count[0]
    )
    columns = state.reshape(patches, -1, members)
    out = analyse_patches(places, vals.reshape(-1), obs_count[0, 0], ocean_mask[0, 0], tiles, columns)
    return out.reshape(state.shape)


def solution(mesh):
    placed = (
        P("lat", "lon", None, None, None, None),
        P("lat", "lon", None, None),
        P("lat", "lon", None, None),
        P("lat", "lon", None),
        P("lat", "lon", None),
        P("lat", "lon", None, None),
        P("lat", "lon", None),
    )
    return jax.shard_map(
        shards,
        mesh=mesh,
        in_specs=placed,
        out_specs=P("lat", "lon", None, None, None, None),
        check_vma=False,
    )
```
